32 devices in a mesh: parts: 2 (over y), pencil: 4 (over z), slab: 2 (over x), field: 2 (over core).
Axes of the slice: x: 2, y: 2, z: 4, core: 2. Of those that a mesh axis runs over, the one named last changes fastest.
Arguments:
- state: bfloat16 [16, 2, 512, 512], P('parts', 'slab', 'pencil'), parts along dimension 0, may hold values from -6 to 6
- tangents: bfloat16 [16, 8, 2, 512, 512], P(('parts', 'field'), None, 'slab', 'pencil'), parts along dimension 0, may hold values from -6 to 6
- d1: bfloat16 [512, 512], replicated, may hold values from -0.25 to 0.25
- d2: bfloat16 [512, 512], replicated, may hold values from -0.25 to 0.25
- filt: bfloat16 [512, 512], replicated, may hold values from -0.25 to 0.25
- advect: float32 [2, 8], replicated, may hold values from 0.3 to 1
- diffuse: float32 [8], replicated, may hold values from 0.3 to 1
- coef: float32 [8, 8], replicated, may hold values from -3 to 3
- rates: float32 [8, 8], replicated, may hold values from -3.6 to 3.6
Outputs:
- state_out: bfloat16 [16, 2, 512, 512], P('parts', 'slab', 'pencil'), parts along dimension 0
- tangent_out: bfloat16 [16, 8, 2, 512, 512], P(('parts', 'field'), None, 'slab', 'pencil'), parts along dimension 0
The draws below stay inside these ranges and needn't reach their ends.
There are 2 independent parts, one for each index of `parts`. The reference program is written for one: setup_inputs(seed, part) draws one part's arguments, and reference() takes and returns one part's arrays. A program takes and returns all parts, laid end to end along the dimension named above; an argument that names none is the same for every part. Nothing has to cross between parts.
All inputs are finite; a program needn't handle non-finite values.
Results may differ from the reference program's by a relative error of at most 0.0094.
Values may be sent and summed in bfloat16 or wider, within the bound.
A program may use at most 128 MiB of HBM per device.

```python
import jax
import jax.numpy as jnp
from jax import lax

N = 512
S = 8
K = 8
STEPS = 1
NZ = 2


def steps_of(key, dims, cuts, low, high):
    factor_of = 1.0
    for dim, blocks in cuts:
        draws = jax.random.uniform(jax.random.fold_in(jax.random.fold_in(key, 6), dim), (blocks,), jnp.float32, low / len(cuts), high / len(cuts))
        factor_of = factor_of * jnp.repeat(jnp.exp(draws), dims[dim] // blocks).reshape((-1,) + (1,) * (len(dims) - 1 - dim))
    return factor_of


def scatter_about(key, extent, width, most, cuts=(), kind=jnp.bfloat16):
    array = width * jax.random.normal(key, extent, jnp.float32)
    if cuts:
        array = array * steps_of(key, extent, cuts, -0.22, 0.18)
    return jnp.clip(array, -most, most).astype(kind)


def setup_inputs(seed: int = 0, part: int = 0) -> dict:
    keys = jax.random.split(jax.random.key(seed), 10)
    own_keys = jax.random.split(jax.random.fold_in(keys[9], part), 10)
    state = scatter_about(own_keys[0], (S, NZ, N, N), 1.0, 6.0, ((1, 2), (2, 4)))
    tangents = scatter_about(own_keys[1], (K, S, NZ, N, N), 1.0, 6.0, ((0, 2), (2, 2), (3, 4)))
    d1 = scatter_about(keys[2], (N, N), N ** -0.5, 0.25)
    d2 = scatter_about(keys[3], (N, N), N ** -0.5, 0.25)
    filt = scatter_about(keys[4], (N, N), N ** -0.5, 0.25)
    advect = jnp.clip(jax.random.uniform(keys[5], (2, S), jnp.float32, 0.3, 1.0), 0.3, 1.0)
    diffuse = jnp.clip(jax.random.uniform(keys[6], (S,), jnp.float32, 0.3, 1.0), 0.3, 1.0)
    coef = scatter_about(keys[7], (K, S), 0.5, 3.0, (), jnp.float32)
    rates = scatter_about(keys[8], (K, S), 0.6, 3.6, (), jnp.float32)
    return {"state": state, "tangents": tangents, "d1": d1, "d2": d2, "filt": filt, "advect": advect, "diffuse": diffuse, "coef": coef, "rates": rates}


highest = lax.Precision.HIGHEST
time_step = 0.4


def spread(values, fields):
    return values.reshape(values.shape + (1,) * (fields.ndim - values.ndim))


def reaction(state, tangent, coef, rates, offset):
    state_float = state.astype(jnp.float32)
    argument = jnp.einsum('ps,s...->p...', rates, state_float, precision=highest)
    activity = jnp.tanh(argument)
    slopes = 1.0 - activity * activity
    state_rate = jnp.einsum('ps,p...->s...', coef, activity, precision=highest)
    tangent_float = tangent.astype(jnp.float32)
    mixing = jnp.einsum('pt,qt...->qp...', rates, tangent_float, precision=highest)
    number = tangent.shape[0]
    own_coef = lax.dynamic_slice_in_dim(coef, offset, number, 0)
    own_activity = lax.dynamic_slice_in_dim(activity, offset, number, 0)
    tangent_rate = jnp.einsum('ps,qp...->qs...', coef, slopes[None] * mixing, precision=highest)
    tangent_rate = tangent_rate + spread(own_coef, tangent) * own_activity[:, None]
    return state_rate, tangent_rate


def update(fields, rate, speeds, diffusivity, operators):
    derivative_op, diffusion_op, filter_op = operators
    slope_term = jnp.dot(fields, derivative_op, preferred_element_type=jnp.float32)
    curve_term = jnp.dot(fields, diffusion_op, preferred_element_type=jnp.float32)
    middle = fields.astype(jnp.float32) + time_step * (
        spread(diffusivity, fields) * curve_term - spread(speeds, fields) * slope_term + rate)
    middle = middle.astype(jnp.bfloat16)
    return jnp.dot(middle, filter_op, preferred_element_type=jnp.float32).astype(jnp.bfloat16)


def reference(state, tangents, d1, d2, filt, advect, diffuse, coef, rates):
    operators = (d1, d2, filt)

    def plane(pair):
        plane_state, plane_tangent = pair
        for section in range(STEPS):
            for direction in range(2):
                speeds = advect[direction]
                state_rate, tangent_rate = reaction(plane_state, plane_tangent, coef, rates, 0)
                plane_tangent = update(plane_tangent, tangent_rate, speeds[None, :], diffuse[None, :], operators)
                plane_state = update(plane_state, state_rate, speeds, diffuse, operators)
                plane_state = jnp.swapaxes(plane_state, -1, -2)
                plane_tangent = jnp.swapaxes(plane_tangent, -1, -2)
        return plane_state, plane_tangent

    result_state, result_tangent = lax.map(plane, (jnp.moveaxis(state, 1, 0), jnp.moveaxis(tangents, 2, 0)))
    return jnp.moveaxis(result_state, 0, 1), jnp.moveaxis(result_tangent, 0, 2)
```

```python
import functools

import jax
import jax.numpy as jnp
from jax import lax
from jax.experimental import pallas as pl
from jax.experimental.pallas import tpu as pltpu
from jax.sharding import PartitionSpec as P

time_step = 0.4
MESH = pl.DeviceIdType.MESH
highest = lax.Precision.HIGHEST


def product(left, right):
    return jnp.dot(left, right, preferred_element_type=jnp.float32)


def kernel(
    n, cores, step,
    state_ref, tangent_ref, d1_ref, d2_ref, filt_ref, advect_ref, diffuse_ref, coef_ref, rates_ref,
    state_out, tangent_out,
    rates_hi, rates_lo, coef_mix, coef_own, act, slopes, lines, state_lines, state_end,
    send_s, send_t, take_s, take_t,
    send_sem, take_sem, pass_send, pass_take,
):
    params, count, rows, length = tangent_ref.shape
    width = length // n
    own = count // cores
    me = lax.axis_index("pencil")
    core = lax.axis_index("field")
    first = core * own

    barrier = pltpu.get_barrier_semaphore()
    for d in range(1, n):
        pl.semaphore_signal(barrier, inc=1, device_id={"pencil": lax.rem(me + d, n)}, device_id_type=MESH)
    for d in range(1, cores):
        pl.semaphore_signal(barrier, inc=1, device_id={"field": lax.rem(core + d, cores)}, device_id_type=MESH)

    def picks(height, offset):
        field = lax.broadcasted_iota(jnp.int32, (height, count), 1)
        row = lax.broadcasted_iota(jnp.int32, (height, count), 0)
        return jnp.where(row // step + offset == field, 1.0, 0.0).astype(jnp.float32)

    def spread(matrix, left, right):
        wide = jnp.dot(left, matrix, precision=highest, preferred_element_type=jnp.float32)
        wide = lax.dot_general(wide, right, (((1,), (1,)), ((), ())), precision=highest, preferred_element_type=jnp.float32)
        cell = lax.broadcasted_iota(jnp.int32, wide.shape, 0) % step
        other = lax.broadcasted_iota(jnp.int32, wide.shape, 1) % step
        return jnp.where(cell == other, wide, 0.0)

    all_picks = picks(count * step, 0)
    own_picks = picks(own * step, first)
    rates_wide = spread(rates_ref[...], all_picks, all_picks)
    rates_hi[...] = rates_wide.astype(jnp.bfloat16)
    rates_lo[...] = (rates_wide - rates_hi[...].astype(jnp.float32)).astype(jnp.bfloat16)
    scaled = time_step * coef_ref[...].T
    coef_mix[...] = spread(scaled, all_picks, all_picks).astype(jnp.bfloat16)
    coef_own[...] = spread(scaled, own_picks, all_picks).astype(jnp.bfloat16)

    def rows_of(values, chosen):
        return time_step * jnp.sum(chosen * values, axis=1, keepdims=True)

    pl.semaphore_wait(barrier, n - 1 + cores - 1)

    def move(leg, group, send, take, d):
        dest = lax.rem(me + d, n)
        if d == 0:
            return pltpu.make_async_copy(send.at[me], take.at[me], take_sem.at[leg, group, 0])
        return pltpu.make_async_remote_copy(
            src_ref=send.at[dest], dst_ref=take.at[me],
            send_sem=send_sem.at[leg, group, d], recv_sem=take_sem.at[leg, group, d],
            device_id={"pencil": dest}, device_id_type=MESH,
        )

    def state_move(leg, d):
        return move(leg, 0, send_s.at[leg], take_s.at[leg, core], d)

    def tangent_move(leg, q, d):
        return move(leg, q + 1, send_t.at[leg, q], take_t.at[leg, q], d)

    def arrived(copy, d):
        if d == 0:
            copy.wait()
        else:
            copy.wait_recv()

    def hand_on(which, ref, d):
        return pltpu.make_async_remote_copy(
            src_ref=ref, dst_ref=ref, send_sem=pass_send.at[which, d], recv_sem=pass_take.at[which, d],
            device_id={"field": lax.rem(core + d, cores)}, device_id_type=MESH,
        )

    def finish(fields, rate, speed, spreading, target):
        slope = product(fields, d1_ref[...])
        curve = product(fields, d2_ref[...])
        middle = fields.astype(jnp.float32) + spreading * curve - speed * slope + rate
        result = product(middle.astype(jnp.bfloat16), filt_ref[...]).astype(jnp.bfloat16)
        for j in range(n):
            target(j, result[:, j * width : (j + 1) * width])

    def state_pass(leg, source):
        speed = rows_of(advect_ref[leg : leg + 1, :], own_picks)
        spreading = rows_of(diffuse_ref[...], own_picks)

        @pl.loop(0, rows // step)
        def _(c):
            part = pl.ds(pl.multiple_of(c * step, step), step)
            fields = source[:, part, :].reshape(count * step, length)
            argument = product(rates_hi[...], fields) + product(rates_lo[...], fields)
            activity = jnp.tanh(argument)
            act[c] = activity
            slopes[c] = 1.0 - activity * activity
            rate = product(coef_own[...], activity.astype(jnp.bfloat16))

            def target(j, block):
                send_s[leg, j, :, part, :] = block.reshape(own, step, width)

            mine = source[pl.ds(first, own), part, :].reshape(own * step, length)
            finish(mine, rate, speed, spreading, target)

        for d in range(n):
            state_move(leg, d).start()

    def tangent_pass(leg, q, source):
        speed = rows_of(advect_ref[leg : leg + 1, :], all_picks)
        spreading = rows_of(diffuse_ref[...], all_picks)

        @pl.loop(0, rows // step)
        def _(c):
            part = pl.ds(pl.multiple_of(c * step, step), step)
            fields = source[:, part, :].reshape(count * step, length)
            mixing = product(rates_hi[...], fields)
            channel = lax.broadcasted_iota(jnp.int32, mixing.shape, 0) // step
            direct = jnp.where(channel == core * params + q, act[c], 0.0)
            rate = product(coef_mix[...], (slopes[c] * mixing + direct).astype(jnp.bfloat16))

            def target(j, block):
                send_t[leg, q, j, :, part, :] = block.reshape(count, step, width)

            finish(fields, rate, speed, spreading, target)

        for d in range(n):
            tangent_move(leg, q, d).start()

    def turned(blocks):
        return blocks.reshape(n * blocks.shape[1], width).T

    state_pass(0, state_ref)

    @pl.loop(0, params)
    def _(q):
        tangent_pass(0, q, tangent_ref.at[q])

    for d in range(n):
        arrived(state_move(0, d), d)
    for d in range(1, cores):
        hand_on(0, take_s.at[0, core], d).start()
    for d in range(1, cores):
        hand_on(0, take_s.at[0, core], d).wait_recv()

    @pl.loop(0, cores)
    def _(h):
        @pl.loop(0, own)
        def _(s):
            state_lines[h * own + s] = turned(take_s[0, h, :, s])

    state_pass(1, state_lines)

    @pl.loop(0, params)
    def _(q):
        for d in range(n):
            arrived(tangent_move(0, q, d), d)

        @pl.loop(0, count)
        def _(s):
            lines[s] = turned(take_t[0, q, :, s])

        tangent_pass(1, q, lines)

    for d in range(n):
        arrived(state_move(1, d), d)

    @pl.loop(0, own)
    def _(s):
        state_end[first + s] = turned(take_s[1, core, :, s])

    for d in range(1, cores):
        hand_on(1, state_end.at[pl.ds(first, own)], d).start()

    @pl.loop(0, params)
    def _(q):
        for d in range(n):
            arrived(tangent_move(1, q, d), d)

        @pl.loop(0, count)
        def _(s):
            tangent_out[q, s] = turned(take_t[1, q, :, s])

    for d in range(1, cores):
        hand_on(1, state_end.at[pl.ds(first, own)], d).wait_recv()
    state_out[...] = state_end[...]

    for leg in range(2):
        for d in range(1, n):
            state_move(leg, d).wait_send()
        for d in range(1, cores):
            hand_on(0, take_s.at[0, core], d).wait_send() if leg == 0 else hand_on(
                1, state_end.at[pl.ds(first, own)], d
            ).wait_send()

        @pl.loop(0, params)
        def _(q):
            for d in range(1, n):
                tangent_move(leg, q, d).wait_send()


def local(n, cores, state, tangents, d1, d2, filt, advect, diffuse, coef, rates):
    params, count, planes, rows, length = tangents.shape
    step = 32 if rows % 32 == 0 else rows
    width = length // n
    own = count // cores
    bf16, f32 = jnp.bfloat16, jnp.float32
    spot = pl.BlockSpec(memory_space=pltpu.VMEM)
    cells = params * count * rows * length
    call = pl.pallas_call(
        functools.partial(kernel, n, cores, step),
        out_shape=(
            jax.ShapeDtypeStruct((count, rows, length), bf16),
            jax.ShapeDtypeStruct((params, count, rows, length), bf16),
        ),
        in_specs=[spot] * 9,
        out_specs=(spot, spot),
        scratch_shapes=[
            pltpu.VMEM((count * step, count * step), bf16),
            pltpu.VMEM((count * step, count * step), bf16),
            pltpu.VMEM((count * step, count * step), bf16),
            pltpu.VMEM((own * step, count * step), bf16),
            pltpu.VMEM((rows // step, count * step, length), f32),
            pltpu.VMEM((rows // step, count * step, length), f32),
            pltpu.VMEM((count, width, length), bf16),
            pltpu.VMEM((count, width, length), bf16),
            pltpu.VMEM((count, rows, length), bf16),
            pltpu.VMEM((2, n, own, rows, width), bf16),
            pltpu.VMEM((2, params, n, count, rows, width), bf16),
            pltpu.VMEM((2, cores, n, own, rows, width), bf16),
            pltpu.VMEM((2, params, n, count, rows, width), bf16),
            pltpu.SemaphoreType.DMA((2, params + 1, n)),
            pltpu.SemaphoreType.DMA((2, params + 1, n)),
            pltpu.SemaphoreType.DMA((2, cores)),
            pltpu.SemaphoreType.DMA((2, cores)),
        ],
        compiler_params=pltpu.CompilerParams(
            collective_id=0, has_side_effects=True, vmem_limit_bytes=56 * 2**20
        ),
        cost_estimate=pl.CostEstimate(
            flops=cells * length * 12, bytes_accessed=cells * 4, transcendentals=count * rows * length * 2
        ),
    )
    outs = [
        call(state[:, z], tangents[:, :, z], d1, d2, filt, advect, diffuse[None, :], coef, rates)
        for z in range(planes)
    ]
    return jnp.stack([o[0] for o in outs], 1), jnp.stack([o[1] for o in outs], 2)


def solution(mesh):
    lines = P("parts", "slab", "pencil", None)
    tangent_lines = P(("parts", "field"), None, "slab", "pencil", None)
    return jax.shard_map(
        functools.partial(local, mesh.shape["pencil"], mesh.shape["field"]),
        mesh=mesh,
        in_specs=(lines, tangent_lines) + (P(),) * 7,
        out_specs=(lines, tangent_lines),
        check_vma=False,
    )
```

```python
import functools

import jax
import jax.numpy as jnp
from jax import lax
from jax.experimental import pallas as pl
from jax.experimental.pallas import tpu as pltpu
from jax.sharding import PartitionSpec as P

time_step = 0.4
MESH = pl.DeviceIdType.MESH
highest = lax.Precision.HIGHEST


def product(left, right):
    return jnp.dot(left, right, preferred_element_type=jnp.float32)


def kernel(
    n, cores, step,
    state_in, tangent_in, d1_in, d2_in, filt_in, advect_ref, diffuse_ref, coef_ref, rates_ref,
    state_out, tangent_out,
    state_ref, tangent_ref, d1_ref, d2_ref, filt_ref, tangent_end,
    rates_hi, rates_lo, coef_mix, coef_own, act, slopes, lines, state_lines, state_end,
    send_s, send_t, take_s, take_t,
    send_sem, take_sem, pass_send, pass_take, load_sem, store_sem,
):
    params, count, rows, length = tangent_ref.shape
    width = length // n
    own = count // cores
    me = lax.axis_index("pencil")
    core = lax.axis_index("field")
    first = core * own
    order = sorted(range(n), key=lambda d: -min(d, n - d))

    barrier = pltpu.get_barrier_semaphore()
    for d in range(1, n):
        pl.semaphore_signal(barrier, inc=1, device_id={"pencil": lax.rem(me + d, n)}, device_id_type=MESH)
    for d in range(1, cores):
        pl.semaphore_signal(barrier, inc=1, device_id={"field": lax.rem(core + d, cores)}, device_id_type=MESH)

    def load(k):
        pairs = ((state_in, state_ref), (d1_in, d1_ref), (d2_in, d2_ref), (filt_in, filt_ref))
        return pltpu.make_async_copy(*pairs[k], load_sem.at[k])

    def tangent_load(q):
        return pltpu.make_async_copy(tangent_in.at[q], tangent_ref.at[q], load_sem.at[4 + q])

    def tangent_store(q):
        return pltpu.make_async_copy(tangent_end.at[q], tangent_out.at[q], store_sem.at[1 + q])

    for k in range(4):
        load(k).start()
    for q in range(params):
        tangent_load(q).start()

    def picks(height, offset):
        field = lax.broadcasted_iota(jnp.int32, (height, count), 1)
        row = lax.broadcasted_iota(jnp.int32, (height, count), 0)
        return jnp.where(row // step + offset == field, 1.0, 0.0).astype(jnp.float32)

    def spread(matrix, left, right):
        wide = jnp.dot(left, matrix, precision=highest, preferred_element_type=jnp.float32)
        wide = lax.dot_general(wide, right, (((1,), (1,)), ((), ())), precision=highest, preferred_element_type=jnp.float32)
        cell = lax.broadcasted_iota(jnp.int32, wide.shape, 0) % step
        other = lax.broadcasted_iota(jnp.int32, wide.shape, 1) % step
        return jnp.where(cell == other, wide, 0.0)

    all_picks = picks(count * step, 0)
    own_picks = picks(own * step, first)
    rates_wide = spread(rates_ref[...], all_picks, all_picks)
    rates_hi[...] = rates_wide.astype(jnp.bfloat16)
    rates_lo[...] = (rates_wide - rates_hi[...].astype(jnp.float32)).astype(jnp.bfloat16)
    scaled = time_step * coef_ref[...].T
    coef_mix[...] = spread(scaled, all_picks, all_picks).astype(jnp.bfloat16)
    coef_own[...] = spread(scaled, own_picks, all_picks).astype(jnp.bfloat16)

    def rows_of(values, chosen):
        return time_step * jnp.sum(chosen * values, axis=1, keepdims=True)

    pl.semaphore_wait(barrier, n - 1 + cores - 1)

    def move(leg, group, send, take, d):
        dest = lax.rem(me + d, n)
        if d == 0:
            return pltpu.make_async_copy(send.at[me], take.at[me], take_sem.at[leg, group, 0])
        return pltpu.make_async_remote_copy(
            src_ref=send.at[dest], dst_ref=take.at[me],
            send_sem=send_sem.at[leg, group, d], recv_sem=take_sem.at[leg, group, d],
            device_id={"pencil": dest}, device_id_type=MESH,
        )

    def state_move(leg, d):
        return move(leg, 0, send_s.at[leg], take_s.at[leg, core], d)

    def tangent_move(leg, q, d):
        return move(leg, q + 1, send_t.at[leg, q], take_t.at[leg, q], d)

    def arrived(copy, d):
        if d == 0:
            copy.wait()
        else:
            copy.wait_recv()

    def hand_on(which, ref, d):
        return pltpu.make_async_remote_copy(
            src_ref=ref, dst_ref=ref, send_sem=pass_send.at[which, d], recv_sem=pass_take.at[which, d],
            device_id={"field": lax.rem(core + d, cores)}, device_id_type=MESH,
        )

    def finish(fields, rate, speed, spreading, target):
        slope = product(fields, d1_ref[...])
        curve = product(fields, d2_ref[...])
        middle = fields.astype(jnp.float32) + spreading * curve - speed * slope + rate
        result = product(middle.astype(jnp.bfloat16), filt_ref[...]).astype(jnp.bfloat16)
        for j in range(n):
            target(j, result[:, j * width : (j + 1) * width])

    def state_pass(leg, source):
        speed = rows_of(advect_ref[leg : leg + 1, :], own_picks)
        spreading = rows_of(diffuse_ref[...], own_picks)

        @pl.loop(0, rows // step)
        def _(c):
            part = pl.ds(pl.multiple_of(c * step, step), step)
            fields = source[:, part, :].reshape(count * step, length)
            argument = product(rates_hi[...], fields) + product(rates_lo[...], fields)
            activity = jnp.tanh(argument)
            act[c] = activity
            slopes[c] = 1.0 - activity * activity
            rate = product(coef_own[...], activity.astype(jnp.bfloat16))

            def target(j, block):
                send_s[leg, j, :, part, :] = block.reshape(own, step, width)

            mine = source[pl.ds(first, own), part, :].reshape(own * step, length)
            finish(mine, rate, speed, spreading, target)

        for d in order:
            state_move(leg, d).start()

    def tangent_pass(leg, q, source):
        speed = rows_of(advect_ref[leg : leg + 1, :], all_picks)
        spreading = rows_of(diffuse_ref[...], all_picks)

        @pl.loop(0, rows // step)
        def _(c):
            part = pl.ds(pl.multiple_of(c * step, step), step)
            fields = source[:, part, :].reshape(count * step, length)
            mixing = product(rates_hi[...], fields)
            channel = lax.broadcasted_iota(jnp.int32, mixing.shape, 0) // step
            direct = jnp.where(channel == core * params + q, act[c], 0.0)
            rate = product(coef_mix[...], (slopes[c] * mixing + direct).astype(jnp.bfloat16))

            def target(j, block):
                send_t[leg, q, j, :, part, :] = block.reshape(count, step, width)

            finish(fields, rate, speed, spreading, target)

        for d in order:
            tangent_move(leg, q, d).start()

    def turned(blocks):
        return blocks.reshape(n * blocks.shape[1], width).T

    for k in range(4):
        load(k).wait()
    state_pass(0, state_ref)

    @pl.loop(0, params)
    def _(q):
        tangent_load(q).wait()
        tangent_pass(0, q, tangent_ref.at[q])

    for d in range(n):
        arrived(state_move(0, d), d)
    for d in range(1, cores):
        hand_on(0, take_s.at[0, core], d).start()
    for d in range(1, cores):
        hand_on(0, take_s.at[0, core], d).wait_recv()

    @pl.loop(0, cores)
    def _(h):
        @pl.loop(0, own)
        def _(s):
            state_lines[h * own + s] = turned(take_s[0, h, :, s])

    state_pass(1, state_lines)

    @pl.loop(0, params)
    def _(q):
        for d in range(n):
            arrived(tangent_move(0, q, d), d)

        @pl.loop(0, count)
        def _(s):
            lines[s] = turned(take_t[0, q, :, s])

        tangent_pass(1, q, lines)

    for d in order:
        arrived(state_move(1, d), d)

    @pl.loop(0, own)
    def _(s):
        state_end[first + s] = turned(take_s[1, core, :, s])

    for d in range(1, cores):
        hand_on(1, state_end.at[pl.ds(first, own)], d).start()

    @pl.loop(0, params)
    def _(q):
        for d in range(n):
            arrived(tangent_move(1, q, d), d)

        @pl.loop(0, count)
        def _(s):
            tangent_end[q, s] = turned(take_t[1, q, :, s])

        tangent_store(q).start()

    for d in range(1, cores):
        hand_on(1, state_end.at[pl.ds(first, own)], d).wait_recv()
    state_store = pltpu.make_async_copy(state_end, state_out, store_sem.at[0])
    state_store.start()

    for leg in range(2):
        for d in range(1, n):
            state_move(leg, d).wait_send()
        for d in range(1, cores):
            hand_on(0, take_s.at[0, core], d).wait_send() if leg == 0 else hand_on(
                1, state_end.at[pl.ds(first, own)], d
            ).wait_send()

        @pl.loop(0, params)
        def _(q):
            for d in range(1, n):
                tangent_move(leg, q, d).wait_send()

    state_store.wait()

    @pl.loop(0, params)
    def _(q):
        tangent_store(q).wait()


def hand_over(state_in, tangent_in, state_out, tangent_out, sems):
    pairs = [(state_in, state_out)]
    for q in range(tangent_in.shape[0]):
        pairs.append((tangent_in.at[q], tangent_out.at[q]))
    copies = [pltpu.make_async_copy(*pair, sems.at[k]) for k, pair in enumerate(pairs)]
    for copy in copies:
        copy.start()
    for copy in copies:
        copy.wait()


def local(n, cores, state, tangents, d1, d2, filt, advect, diffuse, coef, rates):
    params, count, planes, rows, length = tangents.shape
    step = 32 if rows % 32 == 0 else rows
    width = length // n
    own = count // cores
    bf16, f32 = jnp.bfloat16, jnp.float32
    spot = pl.BlockSpec(memory_space=pltpu.VMEM)
    far = pl.BlockSpec(memory_space=pl.ANY)
    cells = params * count * rows * length
    call = pl.pallas_call(
        functools.partial(kernel, n, cores, step),
        out_shape=(
            jax.ShapeDtypeStruct((count, rows, length), bf16),
            jax.ShapeDtypeStruct((params, count, rows, length), bf16),
        ),
        in_specs=[far] * 5 + [spot] * 4,
        out_specs=(far, far),
        scratch_shapes=[
            pltpu.VMEM((count, rows, length), bf16),
            pltpu.VMEM((params, count, rows, length), bf16),
            pltpu.VMEM((length, length), bf16),
            pltpu.VMEM((length, length), bf16),
            pltpu.VMEM((length, length), bf16),
            pltpu.VMEM((params, count, rows, length), bf16),
            pltpu.VMEM((count * step, count * step), bf16),
            pltpu.VMEM((count * step, count * step), bf16),
            pltpu.VMEM((count * step, count * step), bf16),
            pltpu.VMEM((own * step, count * step), bf16),
            pltpu.VMEM((rows // step, count * step, length), f32),
            pltpu.VMEM((rows // step, count * step, length), f32),
            pltpu.VMEM((count, width, length), bf16),
            pltpu.VMEM((count, width, length), bf16),
            pltpu.VMEM((count, rows, length), bf16),
            pltpu.VMEM((2, n, own, rows, width), bf16),
            pltpu.VMEM((2, params, n, count, rows, width), bf16),
            pltpu.VMEM((2, cores, n, own, rows, width), bf16),
            pltpu.VMEM((2, params, n, count, rows, width), bf16),
            pltpu.SemaphoreType.DMA((2, params + 1, n)),
            pltpu.SemaphoreType.DMA((2, params + 1, n)),
            pltpu.SemaphoreType.DMA((2, cores)),
            pltpu.SemaphoreType.DMA((2, cores)),
            pltpu.SemaphoreType.DMA((4 + params,)),
            pltpu.SemaphoreType.DMA((1 + params,)),
        ],
        compiler_params=pltpu.CompilerParams(
            collective_id=0, has_side_effects=True, vmem_limit_bytes=56 * 2**20
        ),
        cost_estimate=pl.CostEstimate(
            flops=cells * length * 12, bytes_accessed=cells * 4, transcendentals=count * rows * length * 2
        ),
    )
    copy = pl.pallas_call(
        hand_over,
        out_shape=(
            jax.ShapeDtypeStruct((count, rows, length), bf16),
            jax.ShapeDtypeStruct((params, count, rows, length), bf16),
        ),
        in_specs=[far, far],
        out_specs=(far, far),
        scratch_shapes=[pltpu.SemaphoreType.DMA((1 + params,))],
        compiler_params=pltpu.CompilerParams(vmem_limit_bytes=2**20),
    )
    outs = [
        copy(*call(state[:, z], tangents[:, :, z], d1, d2, filt, advect, diffuse[None, :], coef, rates))
        for z in range(planes)
    ]
    return jnp.stack([o[0] for o in outs], 1), jnp.stack([o[1] for o in outs], 2)


def solution(mesh):
    lines = P("parts", "slab", "pencil", None)
    tangent_lines = P(("parts", "field"), None, "slab", "pencil", None)
    return jax.shard_map(
        functools.partial(local, mesh.shape["pencil"], mesh.shape["field"]),
        mesh=mesh,
        in_specs=(lines, tangent_lines) + (P(),) * 7,
        out_specs=(lines, tangent_lines),
        check_vma=False,
    )
```

```python
import functools

import jax
import jax.numpy as jnp
from jax import lax
from jax.experimental import pallas as pl
from jax.experimental.pallas import tpu as pltpu
from jax.sharding import PartitionSpec as P

time_step = 0.4
MESH = pl.DeviceIdType.MESH
highest = lax.Precision.HIGHEST


def product(left, right):
    return jnp.dot(left, right, preferred_element_type=jnp.float32)


def kernel(
    n, cores, step,
    state_in, tangent_in, d1_in, d2_in, filt_in, advect_ref, diffuse_ref, coef_ref, rates_ref,
    state_out, tangent_out,
    state_ref, tangent_ref, d1_ref, d2_ref, filt_ref, tangent_end,
    rates_hi, rates_lo, coef_mix, coef_own, act, slopes, lines, state_lines, state_end,
    send_s, send_t, take_s, take_t,
    send_sem, take_sem, pass_send, pass_take, load_sem, store_sem,
):
    params, count, rows, length = tangent_ref.shape
    width = length // n
    own = count // cores
    me = lax.axis_index("pencil")
    core = lax.axis_index("field")
    first = core * own
    order = sorted(range(n), key=lambda d: -min(d, n - d))

    barrier = pltpu.get_barrier_semaphore()
    for d in range(1, n):
        pl.semaphore_signal(barrier, inc=1, device_id={"pencil": lax.rem(me + d, n)}, device_id_type=MESH)
    for d in range(1, cores):
        pl.semaphore_signal(barrier, inc=1, device_id={"field": lax.rem(core + d, cores)}, device_id_type=MESH)

    def load(k):
        pairs = ((state_in, state_ref), (d1_in, d1_ref), (d2_in, d2_ref), (filt_in, filt_ref))
        return pltpu.make_async_copy(*pairs[k], load_sem.at[k])

    def tangent_load(q):
        return pltpu.make_async_copy(tangent_in.at[q], tangent_ref.at[q], load_sem.at[4 + q])

    def tangent_store(q):
        return pltpu.make_async_copy(tangent_end.at[q], tangent_out.at[q], store_sem.at[1 + q])

    for k in range(4):
        load(k).start()
    for q in range(params):
        tangent_load(q).start()

    def picks(height, offset):
        field = lax.broadcasted_iota(jnp.int32, (height, count), 1)
        row = lax.broadcasted_iota(jnp.int32, (height, count), 0)
        return jnp.where(row // step + offset == field, 1.0, 0.0).astype(jnp.float32)

    def spread(matrix, left, right):
        wide = jnp.dot(left, matrix, precision=highest, preferred_element_type=jnp.float32)
        wide = lax.dot_general(wide, right, (((1,), (1,)), ((), ())), precision=highest, preferred_element_type=jnp.float32)
        cell = lax.broadcasted_iota(jnp.int32, wide.shape, 0) % step
        other = lax.broadcasted_iota(jnp.int32, wide.shape, 1) % step
        return jnp.where(cell == other, wide, 0.0)

    all_picks = picks(count * step, 0)
    own_picks = picks(own * step, first)
    rates_wide = spread(rates_ref[...], all_picks, all_picks)
    rates_hi[...] = rates_wide.astype(jnp.bfloat16)
    rates_lo[...] = (rates_wide - rates_hi[...].astype(jnp.float32)).astype(jnp.bfloat16)
    scaled = time_step * coef_ref[...].T
    coef_mix[...] = spread(scaled, all_picks, all_picks).astype(jnp.bfloat16)
    coef_own[...] = spread(scaled, own_picks, all_picks).astype(jnp.bfloat16)

    def rows_of(values, chosen):
        return time_step * jnp.sum(chosen * values, axis=1, keepdims=True)

    pl.semaphore_wait(barrier, n - 1 + cores - 1)

    def move(leg, group, send, take, d):
        dest = lax.rem(me + d, n)
        if d == 0:
            return pltpu.make_async_copy(send.at[me], take.at[me], take_sem.at[leg, group, 0])
        return pltpu.make_async_remote_copy(
            src_ref=send.at[dest], dst_ref=take.at[me],
            send_sem=send_sem.at[leg, group, d], recv_sem=take_sem.at[leg, group, d],
            device_id={"pencil": dest}, device_id_type=MESH,
        )

    def state_move(leg, d):
        return move(leg, 0, send_s.at[leg], take_s.at[leg, core], d)

    def tangent_move(leg, q, d):
        return move(leg, q + 1, send_t.at[leg, q], take_t.at[leg, q], d)

    def arrived(copy, d):
        if d == 0:
            copy.wait()
        else:
            copy.wait_recv()

    def hand_on(which, ref, d):
        return pltpu.make_async_remote_copy(
            src_ref=ref, dst_ref=ref, send_sem=pass_send.at[which, d], recv_sem=pass_take.at[which, d],
            device_id={"field": lax.rem(core + d, cores)}, device_id_type=MESH,
        )

    def finish(fields, rate, speed, spreading, target):
        slope = product(fields, d1_ref[...])
        curve = product(fields, d2_ref[...])
        middle = fields.astype(jnp.float32) + spreading * curve - speed * slope + rate
        result = product(middle.astype(jnp.bfloat16), filt_ref[...]).astype(jnp.bfloat16)
        for j in range(n):
            target(j, result[:, j * width : (j + 1) * width])

    def state_sent(leg):
        for d in range(1, n):
            state_move(leg, d).wait_send()

    def tangent_sent(leg, q):
        for d in range(1, n):
            tangent_move(leg, q, d).wait_send()

    def state_pass(leg, source):
        speed = rows_of(advect_ref[leg : leg + 1, :], own_picks)
        spreading = rows_of(diffuse_ref[...], own_picks)

        @pl.loop(0, rows // step)
        def _(c):
            part = pl.ds(pl.multiple_of(c * step, step), step)
            fields = source[:, part, :].reshape(count * step, length)
            argument = product(rates_hi[...], fields) + product(rates_lo[...], fields)
            activity = jnp.tanh(argument)
            act[c] = activity
            slopes[c] = 1.0 - activity * activity
            rate = product(coef_own[...], activity.astype(jnp.bfloat16))

            def target(j, block):
                send_s[leg, j, :, part, :] = block.reshape(own, step, width)

            mine = source[pl.ds(first, own), part, :].reshape(own * step, length)
            finish(mine, rate, speed, spreading, target)

        if leg == 1:
            tangent_sent(0, params - 2)
        for d in order:
            state_move(leg, d).start()

    def tangent_pass(leg, q, source):
        speed = rows_of(advect_ref[leg : leg + 1, :], all_picks)
        spreading = rows_of(diffuse_ref[...], all_picks)

        @pl.loop(0, rows // step)
        def _(c):
            part = pl.ds(pl.multiple_of(c * step, step), step)
            fields = source[:, part, :].reshape(count * step, length)
            mixing = product(rates_hi[...], fields)
            channel = lax.broadcasted_iota(jnp.int32, mixing.shape, 0) // step
            direct = jnp.where(channel == core * params + q, act[c], 0.0)
            rate = product(coef_mix[...], (slopes[c] * mixing + direct).astype(jnp.bfloat16))

            def target(j, block):
                send_t[leg, q, j, :, part, :] = block.reshape(count, step, width)

            finish(fields, rate, speed, spreading, target)

        if leg == 1:
            pl.when(q == 0)(lambda: tangent_sent(0, params - 1))
        pl.when(q == 1)(lambda: state_sent(leg))
        pl.when(q > 1)(lambda: tangent_sent(leg, q - 2))
        for d in order:
            tangent_move(leg, q, d).start()

    def turned(blocks):
        return blocks.reshape(n * blocks.shape[1], width).T

    for k in range(4):
        load(k).wait()
    state_pass(0, state_ref)

    @pl.loop(0, params)
    def _(q):
        tangent_load(q).wait()
        tangent_pass(0, q, tangent_ref.at[q])

    for d in range(n):
        arrived(state_move(0, d), d)
    for d in range(1, cores):
        hand_on(0, take_s.at[0, core], d).start()
    for d in range(1, cores):
        hand_on(0, take_s.at[0, core], d).wait_recv()

    @pl.loop(0, cores)
    def _(h):
        @pl.loop(0, own)
        def _(s):
            state_lines[h * own + s] = turned(take_s[0, h, :, s])

    state_pass(1, state_lines)

    @pl.loop(0, params)
    def _(q):
        for d in range(n):
            arrived(tangent_move(0, q, d), d)

        @pl.loop(0, count)
        def _(s):
            lines[s] = turned(take_t[0, q, :, s])

        tangent_pass(1, q, lines)

    for d in order:
        arrived(state_move(1, d), d)

    @pl.loop(0, own)
    def _(s):
        state_end[first + s] = turned(take_s[1, core, :, s])

    for d in range(1, cores):
        hand_on(1, state_end.at[pl.ds(first, own)], d).start()

    @pl.loop(0, params)
    def _(q):
        for d in range(n):
            arrived(tangent_move(1, q, d), d)

        @pl.loop(0, count)
        def _(s):
            tangent_end[q, s] = turned(take_t[1, q, :, s])

        tangent_store(q).start()

    for d in range(1, cores):
        hand_on(1, state_end.at[pl.ds(first, own)], d).wait_recv()
    state_store = pltpu.make_async_copy(state_end, state_out, store_sem.at[0])
    state_store.start()

    for q in (params - 2, params - 1):
        tangent_sent(1, q)
    for d in range(1, cores):
        hand_on(0, take_s.at[0, core], d).wait_send()
        hand_on(1, state_end.at[pl.ds(first, own)], d).wait_send()

    state_store.wait()

    @pl.loop(0, params)
    def _(q):
        tangent_store(q).wait()


def hand_over(state_in, tangent_in, state_out, tangent_out, sems):
    pairs = [(state_in, state_out)]
    for q in range(tangent_in.shape[0]):
        pairs.append((tangent_in.at[q], tangent_out.at[q]))
    copies = [pltpu.make_async_copy(*pair, sems.at[k]) for k, pair in enumerate(pairs)]
    for copy in copies:
        copy.start()
    for copy in copies:
        copy.wait()


def local(n, cores, state, tangents, d1, d2, filt, advect, diffuse, coef, rates):
    params, count, planes, rows, length = tangents.shape
    step = 32 if rows % 32 == 0 else rows
    width = length // n
    own = count // cores
    bf16, f32 = jnp.bfloat16, jnp.float32
    spot = pl.BlockSpec(memory_space=pltpu.VMEM)
    far = pl.BlockSpec(memory_space=pl.ANY)
    cells = params * count * rows * length
    call = pl.pallas_call(
        functools.partial(kernel, n, cores, step),
        out_shape=(
            jax.ShapeDtypeStruct((count, rows, length), bf16),
            jax.ShapeDtypeStruct((params, count, rows, length), bf16),
        ),
        in_specs=[far] * 5 + [spot] * 4,
        out_specs=(far, far),
        scratch_shapes=[
            pltpu.VMEM((count, rows, length), bf16),
            pltpu.VMEM((params, count, rows, length), bf16),
            pltpu.VMEM((length, length), bf16),
            pltpu.VMEM((length, length), bf16),
            pltpu.VMEM((length, length), bf16),
            pltpu.VMEM((params, count, rows, length), bf16),
            pltpu.VMEM((count * step, count * step), bf16),
            pltpu.VMEM((count * step, count * step), bf16),
            pltpu.VMEM((count * step, count * step), bf16),
            pltpu.VMEM((own * step, count * step), bf16),
            pltpu.VMEM((rows // step, count * step, length), f32),
            pltpu.VMEM((rows // step, count * step, length), f32),
            pltpu.VMEM((count, width, length), bf16),
            pltpu.VMEM((count, width, length), bf16),
            pltpu.VMEM((count, rows, length), bf16),
            pltpu.VMEM((2, n, own, rows, width), bf16),
            pltpu.VMEM((2, params, n, count, rows, width), bf16),
            pltpu.VMEM((2, cores, n, own, rows, width), bf16),
            pltpu.VMEM((2, params, n, count, rows, width), bf16),
            pltpu.SemaphoreType.DMA((2, params + 1, n)),
            pltpu.SemaphoreType.DMA((2, params + 1, n)),
            pltpu.SemaphoreType.DMA((2, cores)),
            pltpu.SemaphoreType.DMA((2, cores)),
            pltpu.SemaphoreType.DMA((4 + params,)),
            pltpu.SemaphoreType.DMA((1 + params,)),
        ],
        compiler_params=pltpu.CompilerParams(
            collective_id=0, has_side_effects=True, vmem_limit_bytes=56 * 2**20
        ),
        cost_estimate=pl.CostEstimate(
            flops=cells * length * 12, bytes_accessed=cells * 4, transcendentals=count * rows * length * 2
        ),
    )
    copy = pl.pallas_call(
        hand_over,
        out_shape=(
            jax.ShapeDtypeStruct((count, rows, length), bf16),
            jax.ShapeDtypeStruct((params, count, rows, length), bf16),
        ),
        in_specs=[pl.BlockSpec(memory_space=pltpu.HBM)] * 2,
        out_specs=(far, far),
        scratch_shapes=[pltpu.SemaphoreType.DMA((1 + params,))],
        compiler_params=pltpu.CompilerParams(vmem_limit_bytes=2**20),
    )
    outs = [
        copy(*call(state[:, z], tangents[:, :, z], d1, d2, filt, advect, diffuse[None, :], coef, rates))
        for z in range(planes)
    ]
    return jnp.stack([o[0] for o in outs], 1), jnp.stack([o[1] for o in outs], 2)


def solution(mesh):
    lines = P("parts", "slab", "pencil", None)
    tangent_lines = P(("parts", "field"), None, "slab", "pencil", None)
    return jax.shard_map(
        functools.partial(local, mesh.shape["pencil"], mesh.shape["field"]),
        mesh=mesh,
        in_specs=(lines, tangent_lines) + (P(),) * 7,
        out_specs=(lines, tangent_lines),
        check_vma=False,
    )
```

```python
import functools

import jax
import jax.numpy as jnp
from jax import lax
from jax.experimental import pallas as pl
from jax.experimental.pallas import tpu as pltpu
from jax.sharding import PartitionSpec as P

time_step = 0.4
MESH = pl.DeviceIdType.MESH
highest = lax.Precision.HIGHEST


def product(left, right):
    return jnp.dot(left, right, preferred_element_type=jnp.float32)


def kernel(
    n, cores, step,
    state_in, tangent_in, d1_in, d2_in, filt_in, advect_ref, diffuse_ref, coef_ref, rates_ref,
    state_out, tangent_out,
    state_ref, tangent_ref, d1_ref, d2_ref, filt_ref, tangent_end,
    rates_hi, rates_lo, coef_mix, coef_own, act, slopes, lines, state_lines, state_end,
    send_s, send_t, take_s, take_t,
    send_sem, take_sem, pass_send, pass_take, load_sem, store_sem, part_send, part_take,
):
    params, count, rows, length = tangent_ref.shape
    width = length // n
    own = count // cores
    me = lax.axis_index("pencil")
    core = lax.axis_index("field")
    first = core * own
    order = sorted(range(n), key=lambda d: -min(d, n - d))

    barrier = pltpu.get_barrier_semaphore()
    for d in range(1, n):
        pl.semaphore_signal(barrier, inc=1, device_id={"pencil": lax.rem(me + d, n)}, device_id_type=MESH)
    for d in range(1, cores):
        pl.semaphore_signal(barrier, inc=1, device_id={"field": lax.rem(core + d, cores)}, device_id_type=MESH)

    def load(k):
        pairs = ((state_in, state_ref), (d1_in, d1_ref), (d2_in, d2_ref), (filt_in, filt_ref))
        return pltpu.make_async_copy(*pairs[k], load_sem.at[k])

    def tangent_load(q):
        return pltpu.make_async_copy(tangent_in.at[q], tangent_ref.at[q], load_sem.at[4 + q])

    def tangent_store(q):
        return pltpu.make_async_copy(tangent_end.at[q], tangent_out.at[q], store_sem.at[1 + q])

    for k in range(4):
        load(k).start()
    for q in range(params):
        tangent_load(q).start()

    def picks(height, offset):
        field = lax.broadcasted_iota(jnp.int32, (height, count), 1)
        row = lax.broadcasted_iota(jnp.int32, (height, count), 0)
        return jnp.where(row // step + offset == field, 1.0, 0.0).astype(jnp.float32)

    def spread(matrix, left, right):
        wide = jnp.dot(left, matrix, precision=highest, preferred_element_type=jnp.float32)
        wide = lax.dot_general(wide, right, (((1,), (1,)), ((), ())), precision=highest, preferred_element_type=jnp.float32)
        cell = lax.broadcasted_iota(jnp.int32, wide.shape, 0) % step
        other = lax.broadcasted_iota(jnp.int32, wide.shape, 1) % step
        return jnp.where(cell == other, wide, 0.0)

    all_picks = picks(count * step, 0)
    own_picks = picks(own * step, first)
    rates_wide = spread(rates_ref[...], all_picks, all_picks)
    rates_hi[...] = rates_wide.astype(jnp.bfloat16)
    rates_lo[...] = (rates_wide - rates_hi[...].astype(jnp.float32)).astype(jnp.bfloat16)
    scaled = time_step * coef_ref[...].T
    coef_mix[...] = spread(scaled, all_picks, all_picks).astype(jnp.bfloat16)
    coef_own[...] = spread(scaled, own_picks, all_picks).astype(jnp.bfloat16)

    def rows_of(values, chosen):
        return time_step * jnp.sum(chosen * values, axis=1, keepdims=True)

    pl.semaphore_wait(barrier, n - 1 + cores - 1)

    def move(leg, group, send, take, d):
        dest = lax.rem(me + d, n)
        if d == 0:
            return pltpu.make_async_copy(send.at[me], take.at[me], take_sem.at[leg, group, 0])
        return pltpu.make_async_remote_copy(
            src_ref=send.at[dest], dst_ref=take.at[me],
            send_sem=send_sem.at[leg, group, d], recv_sem=take_sem.at[leg, group, d],
            device_id={"pencil": dest}, device_id_type=MESH,
        )

    def part_move(c, d):
        part = pl.ds(c * step, step)
        dest = lax.rem(me + d, n)
        if d == 0:
            return pltpu.make_async_copy(
                send_s.at[0, me, :, part], take_s.at[0, core, me, :, part], part_take.at[c, 0]
            )
        return pltpu.make_async_remote_copy(
            src_ref=send_s.at[0, dest, :, part], dst_ref=take_s.at[0, core, me, :, part],
            send_sem=part_send.at[c, d], recv_sem=part_take.at[c, d],
            device_id={"pencil": dest}, device_id_type=MESH,
        )

    def state_move(leg, d):
        return move(leg, 0, send_s.at[leg], take_s.at[leg, core], d)

    def tangent_move(leg, q, d):
        return move(leg, q + 1, send_t.at[leg, q], take_t.at[leg, q], d)

    def arrived(copy, d):
        if d == 0:
            copy.wait()
        else:
            copy.wait_recv()

    def hand_on(which, ref, d):
        return pltpu.make_async_remote_copy(
            src_ref=ref, dst_ref=ref, send_sem=pass_send.at[which, d], recv_sem=pass_take.at[which, d],
            device_id={"field": lax.rem(core + d, cores)}, device_id_type=MESH,
        )

    def finish(fields, rate, speed, spreading, target):
        slope = product(fields, d1_ref[...])
        curve = product(fields, d2_ref[...])
        middle = fields.astype(jnp.float32) + spreading * curve - speed * slope + rate
        result = product(middle.astype(jnp.bfloat16), filt_ref[...]).astype(jnp.bfloat16)
        for j in range(n):
            target(j, result[:, j * width : (j + 1) * width])

    def state_sent(leg):
        for d in range(1, n):
            if leg == 1:
                state_move(leg, d).wait_send()
            else:
                for c in range(rows // step):
                    part_move(c, d).wait_send()

    def tangent_sent(leg, q):
        for d in range(1, n):
            tangent_move(leg, q, d).wait_send()

    def state_pass(leg, source):
        speed = rows_of(advect_ref[leg : leg + 1, :], own_picks)
        spreading = rows_of(diffuse_ref[...], own_picks)

        @pl.loop(0, rows // step)
        def _(c):
            part = pl.ds(pl.multiple_of(c * step, step), step)
            fields = source[:, part, :].reshape(count * step, length)
            argument = product(rates_hi[...], fields) + product(rates_lo[...], fields)
            activity = jnp.tanh(argument)
            act[c] = activity
            slopes[c] = 1.0 - activity * activity
            rate = product(coef_own[...], activity.astype(jnp.bfloat16))

            def target(j, block):
                send_s[leg, j, :, part, :] = block.reshape(own, step, width)

            mine = source[pl.ds(first, own), part, :].reshape(own * step, length)
            finish(mine, rate, speed, spreading, target)

            if leg == 0:
                for d in order:
                    part_move(c, d).start()

        if leg == 1:
            tangent_sent(0, params - 2)
            for d in order:
                state_move(leg, d).start()

    def tangent_pass(leg, q, source):
        speed = rows_of(advect_ref[leg : leg + 1, :], all_picks)
        spreading = rows_of(diffuse_ref[...], all_picks)

        @pl.loop(0, rows // step)
        def _(c):
            part = pl.ds(pl.multiple_of(c * step, step), step)
            fields = source[:, part, :].reshape(count * step, length)
            mixing = product(rates_hi[...], fields)
            channel = lax.broadcasted_iota(jnp.int32, mixing.shape, 0) // step
            direct = jnp.where(channel == core * params + q, act[c], 0.0)
            rate = product(coef_mix[...], (slopes[c] * mixing + direct).astype(jnp.bfloat16))

            def target(j, block):
                send_t[leg, q, j, :, part, :] = block.reshape(count, step, width)

            finish(fields, rate, speed, spreading, target)

        if leg == 1:
            pl.when(q == 0)(lambda: tangent_sent(0, params - 1))
        pl.when(q == 1)(lambda: state_sent(leg))
        pl.when(q > 1)(lambda: tangent_sent(leg, q - 2))
        for d in order:
            tangent_move(leg, q, d).start()

    def turned(blocks):
        return blocks.reshape(n * blocks.shape[1], width).T

    for k in range(4):
        load(k).wait()
    state_pass(0, state_ref)

    @pl.loop(0, params)
    def _(q):
        tangent_load(q).wait()
        tangent_pass(0, q, tangent_ref.at[q])

    for d in range(n):
        for c in range(rows // step):
            arrived(part_move(c, d), d)
    for d in range(1, cores):
        hand_on(0, take_s.at[0, core], d).start()
    for d in range(1, cores):
        hand_on(0, take_s.at[0, core], d).wait_recv()

    @pl.loop(0, cores)
    def _(h):
        @pl.loop(0, own)
        def _(s):
            state_lines[h * own + s] = turned(take_s[0, h, :, s])

    state_pass(1, state_lines)

    @pl.loop(0, params)
    def _(q):
        for d in range(n):
            arrived(tangent_move(0, q, d), d)

        @pl.loop(0, count)
        def _(s):
            lines[s] = turned(take_t[0, q, :, s])

        tangent_pass(1, q, lines)

    for d in order:
        arrived(state_move(1, d), d)

    @pl.loop(0, own)
    def _(s):
        state_end[first + s] = turned(take_s[1, core, :, s])

    for d in range(1, cores):
        hand_on(1, state_end.at[pl.ds(first, own)], d).start()

    @pl.loop(0, params)
    def _(q):
        for d in range(n):
            arrived(tangent_move(1, q, d), d)

        @pl.loop(0, count)
        def _(s):
            tangent_end[q, s] = turned(take_t[1, q, :, s])

        tangent_store(q).start()

    for d in range(1, cores):
        hand_on(1, state_end.at[pl.ds(first, own)], d).wait_recv()
    state_store = pltpu.make_async_copy(state_end, state_out, store_sem.at[0])
    state_store.start()

    for q in (params - 2, params - 1):
        tangent_sent(1, q)
    for d in range(1, cores):
        hand_on(0, take_s.at[0, core], d).wait_send()
        hand_on(1, state_end.at[pl.ds(first, own)], d).wait_send()

    state_store.wait()

    @pl.loop(0, params)
    def _(q):
        tangent_store(q).wait()


def hand_over(state_in, tangent_in, state_out, tangent_out, sems):
    pairs = [(state_in, state_out)]
    for q in range(tangent_in.shape[0]):
        pairs.append((tangent_in.at[q], tangent_out.at[q]))
    copies = [pltpu.make_async_copy(*pair, sems.at[k]) for k, pair in enumerate(pairs)]
    for copy in copies:
        copy.start()
    for copy in copies:
        copy.wait()


def local(n, cores, state, tangents, d1, d2, filt, advect, diffuse, coef, rates):
    params, count, planes, rows, length = tangents.shape
    step = 32 if rows % 32 == 0 else rows
    width = length // n
    own = count // cores
    bf16, f32 = jnp.bfloat16, jnp.float32
    spot = pl.BlockSpec(memory_space=pltpu.VMEM)
    far = pl.BlockSpec(memory_space=pl.ANY)
    cells = params * count * rows * length
    call = pl.pallas_call(
        functools.partial(kernel, n, cores, step),
        out_shape=(
            jax.ShapeDtypeStruct((count, rows, length), bf16),
            jax.ShapeDtypeStruct((params, count, rows, length), bf16),
        ),
        in_specs=[far] * 5 + [spot] * 4,
        out_specs=(far, far),
        scratch_shapes=[
            pltpu.VMEM((count, rows, length), bf16),
            pltpu.VMEM((params, count, rows, length), bf16),
            pltpu.VMEM((length, length), bf16),
            pltpu.VMEM((length, length), bf16),
            pltpu.VMEM((length, length), bf16),
            pltpu.VMEM((params, count, rows, length), bf16),
            pltpu.VMEM((count * step, count * step), bf16),
            pltpu.VMEM((count * step, count * step), bf16),
            pltpu.VMEM((count * step, count * step), bf16),
            pltpu.VMEM((own * step, count * step), bf16),
            pltpu.VMEM((rows // step, count * step, length), f32),
            pltpu.VMEM((rows // step, count * step, length), f32),
            pltpu.VMEM((count, width, length), bf16),
            pltpu.VMEM((count, width, length), bf16),
            pltpu.VMEM((count, rows, length), bf16),
            pltpu.VMEM((2, n, own, rows, width), bf16),
            pltpu.VMEM((2, params, n, count, rows, width), bf16),
            pltpu.VMEM((2, cores, n, own, rows, width), bf16),
            pltpu.VMEM((2, params, n, count, rows, width), bf16),
            pltpu.SemaphoreType.DMA((2, params + 1, n)),
            pltpu.SemaphoreType.DMA((2, params + 1, n)),
            pltpu.SemaphoreType.DMA((2, cores)),
            pltpu.SemaphoreType.DMA((2, cores)),
            pltpu.SemaphoreType.DMA((4 + params,)),
            pltpu.SemaphoreType.DMA((1 + params,)),
            pltpu.SemaphoreType.DMA((rows // step, n)),
            pltpu.SemaphoreType.DMA((rows // step, n)),
        ],
        compiler_params=pltpu.CompilerParams(
            collective_id=0, has_side_effects=True, vmem_limit_bytes=56 * 2**20
        ),
        cost_estimate=pl.CostEstimate(
            flops=cells * length * 12, bytes_accessed=cells * 4, transcendentals=count * rows * length * 2
        ),
    )
    copy = pl.pallas_call(
        hand_over,
        out_shape=(
            jax.ShapeDtypeStruct((count, rows, length), bf16),
            jax.ShapeDtypeStruct((params, count, rows, length), bf16),
        ),
        in_specs=[pl.BlockSpec(memory_space=pltpu.HBM)] * 2,
        out_specs=(far, far),
        scratch_shapes=[pltpu.SemaphoreType.DMA((1 + params,))],
        compiler_params=pltpu.CompilerParams(vmem_limit_bytes=60 * 2**20),
    )
    outs = [
        copy(*call(state[:, z], tangents[:, :, z], d1, d2, filt, advect, diffuse[None, :], coef, rates))
        for z in range(planes)
    ]
    return jnp.stack([o[0] for o in outs], 1), jnp.stack([o[1] for o in outs], 2)


def solution(mesh):
    lines = P("parts", "slab", "pencil", None)
    tangent_lines = P(("parts", "field"), None, "slab", "pencil", None)
    return jax.shard_map(
        functools.partial(local, mesh.shape["pencil"], mesh.shape["field"]),
        mesh=mesh,
        in_specs=(lines, tangent_lines) + (P(),) * 7,
        out_specs=(lines, tangent_lines),
        check_vma=False,
    )
```
